32 devices in a mesh: run: 2 (over y), lon: 4 (over z), node: 2 (over x), lev: 2 (over core).
Axes of the slice: x: 2, y: 2, z: 4, core: 2. Of those that a mesh axis runs over, the one named last changes fastest.
Arguments:
- initial_state: float32 [8, 4, 96, 512], P(None, 'lev', 'run', 'lon'), parts along dimension 2, may hold values from -6 to 6
- node_states: float32 [8, 8, 4, 96, 512], P('node', None, 'lev', 'run', 'lon'), parts along dimension 3, may hold values from -6 to 6
- node_order: int32 [8], replicated, may hold values from 0 to 7, each once
- sector_depth: int32 [8, 96], P('node', 'run'), parts along dimension 1, may hold values from 0 to 2, as said below
- cell_offset: int32 [8, 96], P('node', 'run'), parts along dimension 1, may hold values from 2 to 127
- fraction: float32 [8, 96], P('node', 'run'), parts along dimension 1, may hold values from 0 to 1
- reaction_matrix: float32 [8, 8], replicated, may hold values from -2 to 2
- diffusivity: float32 [4], P('lev'), may hold values from 0.1 to 1
Outputs:
- new_states: float32 [8, 8, 4, 96, 512], P('node', None, 'lev', 'run', 'lon'), parts along dimension 3
The draws below stay inside these ranges and needn't reach their ends.
There are 2 independent parts, one for each index of `run`. The reference program is written for one: setup_inputs(seed, part) draws one part's arguments, and reference() takes and returns one part's arrays. A program takes and returns all parts, laid end to end along the dimension named above; an argument that names none is the same for every part. Nothing has to cross between parts.
Inputs may be any that keep to these rules, and one draw needn't show every extreme that they name: `sector_depth`: rows among the 6 nearest either pole have depth 2 or more, all other rows depth 0 or 1; the rows at both poles have depth 2, the middle row depth 0.
All inputs are finite; a program needn't handle non-finite values.
Results may differ from the reference program's by a relative error of at most 0.0003.
Values sent between devices are 32-bit elements; how exact they have to be, the bound alone decides.
A program may use at most 128 MiB of HBM per device.

```python
import math
import jax
import jax.numpy as jnp
import numpy as np
from jax import lax

TR = 8
NODES = 8
NLAT = 48
CL = 128
NLON = 512
LEV = 4
DEPTH_MAX = 2


def draw_sector_depth(key, part):
    first_key = jax.random.fold_in(key, 11)
    second_key = jax.random.fold_in(key, 23)
    shallow = jax.random.randint(first_key, (NODES, NLAT), 0, 2)
    deep = jax.random.randint(second_key, (NODES, NLAT), 2, DEPTH_MAX + 1)
    row_index = jnp.arange(NLAT, dtype=jnp.int32)[None, :]
    band_rows = NLAT // 8
    polar = (row_index < band_rows) | (row_index >= NLAT - band_rows)
    result = jnp.where(polar, deep, shallow)
    result = jnp.where((row_index == 0) | (row_index == NLAT - 1), DEPTH_MAX, result)
    result = jnp.where(row_index == NLAT // 2, 0, result)
    return result.astype(jnp.int32)


def set_ends(values, stream_key, low, high):
    shape = values.shape
    index_at = [jax.random.randint(jax.random.fold_in(stream_key, axis), (), 0, shape[axis]) for axis in range(len(shape))]
    values = values.at[tuple(index_at)].set(low)
    longest = shape.index(max(shape))
    index_at[longest] = (index_at[longest] + 1) % shape[longest]
    return values.at[tuple(index_at)].set(high)


def levels(own_key, extent, split, least, high):
    def one(dim, shards_of):
        draws = jax.random.uniform(jax.random.fold_in(jax.random.fold_in(own_key, 6), dim), (shards_of,), jnp.float32, least / len(split), high / len(split))
        return jnp.repeat(jnp.exp(draws), extent[dim] // shards_of).reshape((-1,) + (1,) * (len(extent) - dim - 1))

    loudness = one(*split[0])
    for cut in split[1:]:
        loudness = loudness * one(*cut)
    return loudness


def noise(rng, shape, spread, most, shards=(), kind=jnp.bfloat16):
    drawn = jax.random.normal(rng, shape, jnp.float32) * spread
    if len(shards) > 0:
        drawn = levels(rng, shape, shards, -0.22, 0.18) * drawn
    return jnp.clip(drawn, min=-most, max=most).astype(kind)


def setup_inputs(seed: int = 0, part: int = 0) -> dict:
    keys = jax.random.split(jax.random.key(seed), 9)
    part_splits = jax.random.split(jax.random.fold_in(keys[8], part), 9)
    initial_state = noise(part_splits[0], (TR, LEV, NLAT, NLON), 1.0, 6.0, ((1, 2), (3, 4)), jnp.float32)
    node_states = noise(part_splits[1], (NODES, TR, LEV, NLAT, NLON), 1.0, 6.0, ((0, 2), (2, 2), (4, 4)), jnp.float32)
    node_order = jax.random.permutation(keys[2], NODES).astype(jnp.int32)
    sector_depth = draw_sector_depth(jax.random.fold_in(jax.random.fold_in(keys[8], part), 71), part)
    cell_offset = set_ends(jax.random.randint(part_splits[4], (NODES, NLAT), 2, CL), jax.random.fold_in(part_splits[4], 1), 2, CL - 1).astype(jnp.int32)
    fraction = jnp.clip(1.0 * jax.random.uniform(part_splits[5], (NODES, NLAT), jnp.float32) ** levels(part_splits[5], (NODES, NLAT), ((0, 2),), -0.2, 0.2), 0.0, 1.0)
    reaction_matrix = noise(keys[6], (TR, TR), TR ** -0.5, 2.0, (), jnp.float32)
    diffusivity = jnp.clip(jnp.exp(math.log(1.0) - 2.3025851 * jax.random.uniform(keys[7], (LEV,), jnp.float32) ** levels(keys[7], (LEV,), ((0, 2),), -0.2, 0.2)), 0.1, 1.0)
    return dict(initial_state=initial_state, node_states=node_states, node_order=node_order, sector_depth=sector_depth, cell_offset=cell_offset, fraction=fraction, reaction_matrix=reaction_matrix, diffusivity=diffusivity)


time_step = 0.5
lobatto_points = [-1.0, -0.8717401485096066, -0.5917001814331423, -0.2092992179024789,
                  0.2092992179024789, 0.5917001814331423, 0.8717401485096066, 1.0]


def lobatto_table():
    points = [(value + 1.0) / 2.0 for value in lobatto_points]
    result_rows = [[0.0] * 8 for m in range(8)]
    for j in range(8):
        poly_coeffs = [1.0]
        for k in range(8):
            if k != j:
                factor = 1.0 / (points[j] - points[k])
                grown = [0.0] * (len(poly_coeffs) + 1)
                for i in range(len(poly_coeffs)):
                    grown[i + 1] = grown[i + 1] + poly_coeffs[i] * factor
                    grown[i] = grown[i] - poly_coeffs[i] * points[k] * factor
                poly_coeffs = grown
        for m in range(8):
            total_value = 0.0
            for i in range(len(poly_coeffs)):
                total_value = total_value + poly_coeffs[i] * points[m] ** (i + 1) / (i + 1)
            result_rows[m][j] = total_value
    return np.array(result_rows)


def cubic_weights(fraction):
    return (-fraction * (fraction - 1.0) * (fraction - 2.0) / 6.0,
            (fraction + 1.0) * (fraction - 1.0) * (fraction - 2.0) / 2.0,
            -(fraction + 1.0) * fraction * (fraction - 2.0) / 2.0,
            (fraction + 1.0) * fraction * (fraction - 1.0) / 6.0)


def section_matrix(node_order):
    onehot = (node_order[:, None] == jnp.arange(NODES, dtype=jnp.int32)[None, :]).astype(jnp.float32)
    quad_values = jnp.asarray(lobatto_table(), jnp.float32)
    left = jnp.dot(onehot, quad_values, precision=lax.Precision.HIGHEST)
    return jnp.dot(left, onehot.T, precision=lax.Precision.HIGHEST)


def reference(initial_state, node_states, node_order, sector_depth, cell_offset, fraction, reaction_matrix, diffusivity):
    padded = jnp.pad(node_states, ((0, 0), (0, 0), (1, 1), (0, 0), (0, 0)), mode="edge")
    curvature = padded[:, :, 2:] - 2.0 * node_states + padded[:, :, :-2]
    reaction = jnp.einsum("ts,mslyx->mtlyx", reaction_matrix, jnp.tanh(node_states), precision=lax.Precision.HIGHEST)
    tendency = reaction + diffusivity[None, None, :, None, None] * curvature
    weights = section_matrix(node_order)
    integral = jnp.einsum("mj,jtlyx->mtlyx", weights, tendency, precision=lax.Precision.HIGHEST)
    sectioned = initial_state[None] + time_step * integral
    shift_cells = (sector_depth * CL + cell_offset).astype(jnp.int32)
    columns = jnp.arange(NLON, dtype=jnp.int32)

    def advect(packed):
        field, shift_row, frac_row = packed
        coeffs = cubic_weights(frac_row)
        total = jnp.zeros_like(field)
        for stencil in range(4):
            position = (columns[None, :] - shift_row[:, None] + (stencil - 1)) % NLON
            position = jnp.broadcast_to(position[None, None], field.shape).astype(jnp.int32)
            total = total + coeffs[stencil][None, None, :, None] * jnp.take_along_axis(field, position, axis=3)
        return total

    return lax.map(advect, (sectioned, shift_cells, fraction))
```

```python
import jax
import jax.numpy as jnp
import numpy as np
from jax import lax
from jax.experimental import pallas as pl
from jax.experimental.pallas import tpu as pltpu
from jax.sharding import PartitionSpec as P

NODES = 8


time_step = 0.5
lobatto_points = [
    -1.0,
    -0.8717401485096066,
    -0.5917001814331423,
    -0.2092992179024789,
    0.2092992179024789,
    0.5917001814331423,
    0.8717401485096066,
    1.0,
]


def padded_2(array, sides, width):
    for axis, dim in sides:
        size, length = (lax.axis_size(axis), array.shape[dim])
        up = [(i, (i + 1) % size) for i in range(size - 1)]
        down = [(j, i) for i, j in up]
        last = lax.slice_in_dim(array, length - width, length, axis=dim)
        first = lax.slice_in_dim(array, 0, width, axis=dim)
        before = lax.ppermute(last, axis, up)
        after = lax.ppermute(first, axis, down)
        array = jnp.concatenate([before, array, after], axis=dim)
    return array


def passed_along(array, axis, by):
    length = lax.axis_size(axis)
    return lax.ppermute(array, axis, [(i, (i + by) % length) for i in range(length)])


def lobatto_table():
    points = [(value + 1.0) / 2.0 for value in lobatto_points]
    result_rows = [[0.0] * 8 for m in range(8)]
    for j in range(8):
        poly_coeffs = [1.0]
        for k in range(8):
            if k != j:
                factor = 1.0 / (points[j] - points[k])
                grown = [0.0] * (len(poly_coeffs) + 1)
                for i in range(len(poly_coeffs)):
                    grown[i + 1] = grown[i + 1] + poly_coeffs[i] * factor
                    grown[i] = grown[i] - poly_coeffs[i] * points[k] * factor
                poly_coeffs = grown
        for m in range(8):
            total_value = 0.0
            for i in range(len(poly_coeffs)):
                total_value = total_value + poly_coeffs[i] * points[m] ** (i + 1) / (i + 1)
            result_rows[m][j] = total_value
    return np.array(result_rows)


def cubic_weights(fraction):
    return (
        -fraction * (fraction - 1.0) * (fraction - 2.0) / 6.0,
        (fraction + 1.0) * (fraction - 1.0) * (fraction - 2.0) / 2.0,
        -(fraction + 1.0) * fraction * (fraction - 2.0) / 2.0,
        (fraction + 1.0) * fraction * (fraction - 1.0) / 6.0,
    )


def section_matrix(node_order):
    onehot = (node_order[:, None] == jnp.arange(NODES, dtype=jnp.int32)[None, :]).astype(
        jnp.float32
    )
    quad_values = jnp.asarray(lobatto_table(), jnp.float32)
    left = jnp.dot(onehot, quad_values, precision=lax.Precision.HIGHEST)
    return jnp.dot(left, onehot.T, precision=lax.Precision.HIGHEST)


def tendency_of(states, reaction_matrix, diffusivity):
    level_count = states.shape[2]
    padded = padded_2(states, (("lev", 2),), 1)
    level_pos = lax.axis_index("lev")
    level_last = lax.axis_size("lev") - 1
    below = padded[:, :, :level_count]
    above = padded[:, :, 2:]
    bottom_level = jnp.where(level_pos == 0, states[:, :, :1], below[:, :, :1])
    below = jnp.concatenate([bottom_level, below[:, :, 1:]], axis=2)
    top_level = jnp.where(
        level_pos == level_last, states[:, :, level_count - 1 :], above[:, :, level_count - 1 :]
    )
    above = jnp.concatenate([above[:, :, : level_count - 1], top_level], axis=2)
    curvature = above - 2.0 * states + below
    reaction = jnp.einsum(
        "ts,mslyx->mtlyx", reaction_matrix, jnp.tanh(states), precision=lax.Precision.HIGHEST
    )
    return reaction + diffusivity[None, None, :, None, None] * curvature


def shifted_window(window, starts, length):
    starts = starts[:, None, None, :, None]
    bit = 1
    while bit < length:
        window = jnp.where((starts & bit) != 0, jnp.roll(window, -bit, axis=4), window)
        bit *= 2
    return window


def advect_rows(sectioned, sector_depth, cell_offset, fraction):
    sector_cells = sectioned.shape[4]
    reach_max = min(4, lax.axis_size("lon") - 2) + 1
    depth_cells = sector_depth[:, None, None, :, None]
    nearer = jnp.where(depth_cells == 0, sectioned, 0.0)
    farther = jnp.zeros_like(sectioned)
    previous = sectioned
    for distance in range(1, reach_max + 1):
        source = previous
        arrived = passed_along(source, "lon", 1)
        previous = arrived
        nearer = nearer + jnp.where(depth_cells == distance, arrived, 0.0)
        farther = farther + jnp.where(depth_cells + 1 == distance, arrived, 0.0)
    window = jnp.concatenate([farther, nearer], axis=4)
    starts = sector_cells - cell_offset - 1
    pieces = shifted_window(window, starts, sector_cells)
    coeffs = cubic_weights(fraction)
    result = jnp.zeros_like(sectioned)
    for stencil in range(4):
        result = (
            result
            + coeffs[stencil][:, None, None, :, None]
            * pieces[:, :, :, :, stencil : stencil + sector_cells]
        )
    return result


def shards(
    initial_state,
    node_states,
    node_order,
    sector_depth,
    cell_offset,
    fraction,
    reaction_matrix,
    diffusivity,
):
    slots = node_states.shape[0]
    weights = section_matrix(node_order)
    node_pos = lax.axis_index("node")
    tendency = tendency_of(node_states, reaction_matrix, diffusivity)
    own_rows = lax.dynamic_slice_in_dim(weights, node_pos * slots, slots, 0)
    integral = jnp.einsum(
        "mj,jtlyx->mtlyx",
        own_rows,
        lax.all_gather(tendency, "node", axis=0, tiled=True),
        precision=lax.Precision.HIGHEST,
    )
    sectioned = initial_state[None] + time_step * integral
    return advect_rows(sectioned, sector_depth, cell_offset, fraction)


MESH = pl.DeviceIdType.MESH
ROWS = 8


def sweep_kernel(
    order_ref,
    quad_ref,
    reaction_ref,
    diff_ref,
    init_ref,
    states_ref,
    depth_ref,
    offset_ref,
    frac_ref,
    out_ref,
    edge,
    part,
    part_in,
    sect,
    far_out,
    far_in,
    row_depth,
    row_offset,
    row_frac,
    edge_s,
    edge_r,
    part_s,
    part_r,
    sect_s,
    sect_r,
    far_s,
    far_r,
):
    slots, tracers, _, nlat, cells = states_ref.shape
    blocks = nlat // ROWS
    chunks = 2 * blocks
    lev = lax.axis_index("lev")
    node = lax.axis_index("node")
    lon = lax.axis_index("lon")
    half = lon // 2
    par = lon % 2
    mate = half * 2 + (1 - par)
    middle = (lon == 1) | (lon == 2)

    barrier = pltpu.get_barrier_semaphore()
    pl.semaphore_signal(barrier, inc=1, device_id={"lev": 1 - lev}, device_id_type=MESH)
    pl.semaphore_signal(barrier, inc=1, device_id={"node": 1 - node}, device_id_type=MESH)
    for step in range(1, 4):
        pl.semaphore_signal(
            barrier, inc=1, device_id={"lon": (lon + step) % 4}, device_id_type=MESH
        )
    pl.semaphore_wait(barrier, 5)

    def edge_copy(block):
        rows = pl.ds(pl.multiple_of(block * ROWS, ROWS), ROWS)
        return pltpu.make_async_remote_copy(
            src_ref=states_ref.at[:, :, 1 - lev, rows, :],
            dst_ref=edge.at[:, :, rows, :],
            send_sem=edge_s.at[block],
            recv_sem=edge_r.at[block],
            device_id={"lev": 1 - lev},
            device_id_type=MESH,
        )

    def part_copy(c):
        return pltpu.make_async_remote_copy(
            src_ref=part.at[c],
            dst_ref=part_in.at[c],
            send_sem=part_s.at[c],
            recv_sem=part_r.at[c],
            device_id={"node": 1 - node},
            device_id_type=MESH,
        )

    def sect_copy(c):
        return pltpu.make_async_remote_copy(
            src_ref=sect.at[par, c],
            dst_ref=sect.at[par, c],
            send_sem=sect_s.at[c],
            recv_sem=sect_r.at[c],
            device_id={"lon": mate},
            device_id_type=MESH,
        )

    def far_copy(which, c):
        return pltpu.make_async_remote_copy(
            src_ref=far_out.at[which, c],
            dst_ref=far_in.at[c],
            send_sem=far_s.at[which, c],
            recv_sem=far_r.at[c],
            device_id={"lon": (1 - half) * 2 + which},
            device_id_type=MESH,
        )

    def start_edge(block, carry):
        edge_copy(block).start()
        return carry

    lax.fori_loop(0, blocks, start_edge, 0)

    diagonal = lax.broadcasted_iota(jnp.int32, (nlat, nlat), 0) == lax.broadcasted_iota(
        jnp.int32, (nlat, nlat), 1
    )
    for a in range(slots):
        for source, target in (
            (depth_ref, row_depth),
            (offset_ref, row_offset),
            (frac_ref, row_frac),
        ):
            line = jnp.broadcast_to(source[a : a + 1, :], (nlat, nlat)).astype(jnp.float32)
            column = jnp.sum(jnp.where(diagonal, line, 0.0), axis=1, keepdims=True)
            target[a] = jnp.broadcast_to(column, (nlat, cells)).astype(target.dtype)

    def place(c):
        block = c // 2
        level = jnp.where(c % 2 == 0, lev, 1 - lev)
        return block, level, pl.ds(pl.multiple_of(block * ROWS, ROWS), ROWS)

    def tendencies(c):
        block, level, rows = place(c)
        outer = c % 2 == 0

        @pl.when(jnp.logical_not(outer))
        def _():
            edge_copy(block).wait_recv()

        coefficient = diff_ref[level]

        def body(outer):
            tend = []
            for m in range(slots):
                own = [states_ref[m, t, level, rows, :] for t in range(tracers)]
                acts = [jnp.tanh(x) for x in own]
                row = []
                for t in range(tracers):
                    beyond = own[t] if outer else edge[m, t, rows, :]
                    near = states_ref[m, t, 1 - level, rows, :]
                    value = coefficient * (near - 2.0 * own[t] + beyond)
                    for s in range(tracers):
                        value = value + reaction_ref[t, s] * acts[s]
                    row.append(value)
                tend.append(row)
            for target in range(2):
                group = jnp.where(target == 0, 1 - node, node)
                for a in range(slots):
                    to = order_ref[group * slots + a]
                    w = [
                        time_step * quad_ref[to, order_ref[node * slots + m]]
                        for m in range(slots)
                    ]
                    for t in range(tracers):
                        value = w[0] * tend[0][t]
                        for m in range(1, slots):
                            value = value + w[m] * tend[m][t]
                        if target == 0:
                            part[c, a, t] = value
                        else:
                            sect[par, c, a, t] = init_ref[t, level, rows, :] + value

        pl.when(outer)(lambda: body(True))
        pl.when(jnp.logical_not(outer))(lambda: body(False))
        part_copy(c).start()

    def section(c):
        part_copy(c).wait_recv()
        sect[par, c] = sect[par, c] + part_in[c]
        sect_copy(c).start()

    def interpolate(c):
        block, level, rows = place(c)
        sect_copy(c).wait_recv()
        lanes = lax.broadcasted_iota(jnp.int32, (ROWS, cells), 1)

        def per_slot(a, carry):
            depth = row_depth[a, rows, :]
            offset = row_offset[a, rows, :]
            coeffs = cubic_weights(row_frac[a, rows, :])
            picks = [(lanes - offset + k) & (cells - 1) for k in range(-1, 3)]
            reach = [
                jnp.where(lanes >= offset - k, depth, depth + 1) for k in range(-1, 3)
            ]

            def weights_of(u):
                rel = [(u - e) & 3 for e in reach]
                return [
                    [jnp.where(r == source, w, 0.0) for r, w in zip(rel, coeffs)]
                    for source in range(2)
                ]

            def total(taps, weights):
                value = None
                for source in range(2):
                    for k in range(4):
                        term = weights[source][k] * taps[source][k]
                        value = term if value is None else value + term
                return value

            def run(with_far):
                own = weights_of(par)
                far = [weights_of(2), weights_of(3)] if with_far else []
                for t in range(tracers):
                    fields = [sect[source, c, a, t] for source in range(2)]
                    taps = [
                        [
                            jnp.take_along_axis(f, p, axis=1, mode="promise_in_bounds")
                            for p in picks
                        ]
                        for f in fields
                    ]
                    out_ref[a, t, level, rows, :] = total(taps, own)
                    for which, weights in enumerate(far):
                        far_out[which, c, a, t] = total(taps, weights)

            pl.when(middle)(lambda: run(True))
            pl.when(jnp.logical_not(middle))(lambda: run(False))
            return carry

        lax.fori_loop(0, slots, per_slot, 0)

        @pl.when(middle)
        def _():
            far_copy(0, c).start()
            far_copy(1, c).start()

    def step(i, carry):
        pl.when(i < chunks)(lambda: tendencies(i))
        pl.when((i >= 1) & (i < chunks + 1))(lambda: section(i - 1))
        pl.when(i >= 2)(lambda: interpolate(i - 2))
        return carry

    lax.fori_loop(0, chunks + 2, step, 0)

    def finish(c, carry):
        block, level, rows = place(c)
        far_copy(0, c).wait_recv()
        out_ref[:, :, level, rows, :] = out_ref[:, :, level, rows, :] + far_in[c]
        return carry

    lax.fori_loop(0, chunks, finish, 0)

    def drain(c, carry):
        part_copy(c).wait_send()
        sect_copy(c).wait_send()

        @pl.when(middle)
        def _():
            far_copy(0, c).wait_send()
            far_copy(1, c).wait_send()

        return carry

    lax.fori_loop(0, chunks, drain, 0)

    def drain_edge(block, carry):
        edge_copy(block).wait_send()
        return carry

    lax.fori_loop(0, blocks, drain_edge, 0)


def kernel_shards(
    initial_state,
    node_states,
    node_order,
    sector_depth,
    cell_offset,
    fraction,
    reaction_matrix,
    diffusivity,
):
    slots, tracers, levels, nlat, cells = node_states.shape
    blocks = nlat // ROWS
    chunks = 2 * blocks
    piece = (slots, tracers, ROWS, cells)
    smem = pl.BlockSpec(memory_space=pltpu.SMEM)
    vmem = pl.BlockSpec(memory_space=pltpu.VMEM)
    f32 = jnp.float32
    dma = pltpu.SemaphoreType.DMA
    return pl.pallas_call(
        sweep_kernel,
        out_shape=jax.ShapeDtypeStruct(node_states.shape, f32),
        in_specs=[smem] * 4 + [vmem] * 5,
        out_specs=vmem,
        scratch_shapes=[
            pltpu.VMEM((slots, tracers, nlat, cells), f32),
            pltpu.VMEM((chunks, *piece), f32),
            pltpu.VMEM((chunks, *piece), f32),
            pltpu.VMEM((2, chunks, *piece), f32),
            pltpu.VMEM((2, chunks, *piece), f32),
            pltpu.VMEM((chunks, *piece), f32),
            pltpu.VMEM((slots, nlat, cells), jnp.int32),
            pltpu.VMEM((slots, nlat, cells), jnp.int32),
            pltpu.VMEM((slots, nlat, cells), f32),
            dma((blocks,)),
            dma((blocks,)),
            dma((chunks,)),
            dma((chunks,)),
            dma((chunks,)),
            dma((chunks,)),
            dma((2, chunks)),
            dma((chunks,)),
        ],
        compiler_params=pltpu.CompilerParams(
            collective_id=0, has_side_effects=True, vmem_limit_bytes=40 * 1024 * 1024
        ),
    )(
        node_order,
        jnp.asarray(lobatto_table(), f32),
        reaction_matrix,
        diffusivity,
        initial_state,
        node_states,
        sector_depth,
        cell_offset,
        fraction,
    )


def solution(mesh):
    in_specs = (
        P(None, "lev", "run", "lon"),
        P("node", None, "lev", "run", "lon"),
        P(),
        P("node", "run"),
        P("node", "run"),
        P("node", "run"),
        P(),
        P("lev"),
    )
    out_specs = P("node", None, "lev", "run", "lon")
    sizes = dict(mesh.shape)
    small = sizes["lon"] == 4 and sizes["node"] == 2 and sizes["lev"] == 2
    body = kernel_shards if small else shards
    return jax.shard_map(body, mesh=mesh, in_specs=in_specs, out_specs=out_specs, check_vma=False)
```

```python
import jax
import jax.numpy as jnp
import numpy as np
from jax import lax
from jax.experimental import pallas as pl
from jax.experimental.pallas import tpu as pltpu
from jax.sharding import PartitionSpec as P

NODES = 8


time_step = 0.5
lobatto_points = [
    -1.0,
    -0.8717401485096066,
    -0.5917001814331423,
    -0.2092992179024789,
    0.2092992179024789,
    0.5917001814331423,
    0.8717401485096066,
    1.0,
]


def padded_2(array, sides, width):
    for axis, dim in sides:
        size, length = (lax.axis_size(axis), array.shape[dim])
        up = [(i, (i + 1) % size) for i in range(size - 1)]
        down = [(j, i) for i, j in up]
        last = lax.slice_in_dim(array, length - width, length, axis=dim)
        first = lax.slice_in_dim(array, 0, width, axis=dim)
        before = lax.ppermute(last, axis, up)
        after = lax.ppermute(first, axis, down)
        array = jnp.concatenate([before, array, after], axis=dim)
    return array


def passed_along(array, axis, by):
    length = lax.axis_size(axis)
    return lax.ppermute(array, axis, [(i, (i + by) % length) for i in range(length)])


def lobatto_table():
    points = [(value + 1.0) / 2.0 for value in lobatto_points]
    result_rows = [[0.0] * 8 for m in range(8)]
    for j in range(8):
        poly_coeffs = [1.0]
        for k in range(8):
            if k != j:
                factor = 1.0 / (points[j] - points[k])
                grown = [0.0] * (len(poly_coeffs) + 1)
                for i in range(len(poly_coeffs)):
                    grown[i + 1] = grown[i + 1] + poly_coeffs[i] * factor
                    grown[i] = grown[i] - poly_coeffs[i] * points[k] * factor
                poly_coeffs = grown
        for m in range(8):
            total_value = 0.0
            for i in range(len(poly_coeffs)):
                total_value = total_value + poly_coeffs[i] * points[m] ** (i + 1) / (i + 1)
            result_rows[m][j] = total_value
    return np.array(result_rows)


def cubic_weights(fraction):
    return (
        -fraction * (fraction - 1.0) * (fraction - 2.0) / 6.0,
        (fraction + 1.0) * (fraction - 1.0) * (fraction - 2.0) / 2.0,
        -(fraction + 1.0) * fraction * (fraction - 2.0) / 2.0,
        (fraction + 1.0) * fraction * (fraction - 1.0) / 6.0,
    )


def section_matrix(node_order):
    onehot = (node_order[:, None] == jnp.arange(NODES, dtype=jnp.int32)[None, :]).astype(
        jnp.float32
    )
    quad_values = jnp.asarray(lobatto_table(), jnp.float32)
    left = jnp.dot(onehot, quad_values, precision=lax.Precision.HIGHEST)
    return jnp.dot(left, onehot.T, precision=lax.Precision.HIGHEST)


def tendency_of(states, reaction_matrix, diffusivity):
    level_count = states.shape[2]
    padded = padded_2(states, (("lev", 2),), 1)
    level_pos = lax.axis_index("lev")
    level_last = lax.axis_size("lev") - 1
    below = padded[:, :, :level_count]
    above = padded[:, :, 2:]
    bottom_level = jnp.where(level_pos == 0, states[:, :, :1], below[:, :, :1])
    below = jnp.concatenate([bottom_level, below[:, :, 1:]], axis=2)
    top_level = jnp.where(
        level_pos == level_last, states[:, :, level_count - 1 :], above[:, :, level_count - 1 :]
    )
    above = jnp.concatenate([above[:, :, : level_count - 1], top_level], axis=2)
    curvature = above - 2.0 * states + below
    reaction = jnp.einsum(
        "ts,mslyx->mtlyx", reaction_matrix, jnp.tanh(states), precision=lax.Precision.HIGHEST
    )
    return reaction + diffusivity[None, None, :, None, None] * curvature


def shifted_window(window, starts, length):
    starts = starts[:, None, None, :, None]
    bit = 1
    while bit < length:
        window = jnp.where((starts & bit) != 0, jnp.roll(window, -bit, axis=4), window)
        bit *= 2
    return window


def advect_rows(sectioned, sector_depth, cell_offset, fraction):
    sector_cells = sectioned.shape[4]
    reach_max = min(4, lax.axis_size("lon") - 2) + 1
    depth_cells = sector_depth[:, None, None, :, None]
    nearer = jnp.where(depth_cells == 0, sectioned, 0.0)
    farther = jnp.zeros_like(sectioned)
    previous = sectioned
    for distance in range(1, reach_max + 1):
        source = previous
        arrived = passed_along(source, "lon", 1)
        previous = arrived
        nearer = nearer + jnp.where(depth_cells == distance, arrived, 0.0)
        farther = farther + jnp.where(depth_cells + 1 == distance, arrived, 0.0)
    window = jnp.concatenate([farther, nearer], axis=4)
    starts = sector_cells - cell_offset - 1
    pieces = shifted_window(window, starts, sector_cells)
    coeffs = cubic_weights(fraction)
    result = jnp.zeros_like(sectioned)
    for stencil in range(4):
        result = (
            result
            + coeffs[stencil][:, None, None, :, None]
            * pieces[:, :, :, :, stencil : stencil + sector_cells]
        )
    return result


def shards(
    initial_state,
    node_states,
    node_order,
    sector_depth,
    cell_offset,
    fraction,
    reaction_matrix,
    diffusivity,
):
    slots = node_states.shape[0]
    weights = section_matrix(node_order)
    node_pos = lax.axis_index("node")
    tendency = tendency_of(node_states, reaction_matrix, diffusivity)
    own_rows = lax.dynamic_slice_in_dim(weights, node_pos * slots, slots, 0)
    integral = jnp.einsum(
        "mj,jtlyx->mtlyx",
        own_rows,
        lax.all_gather(tendency, "node", axis=0, tiled=True),
        precision=lax.Precision.HIGHEST,
    )
    sectioned = initial_state[None] + time_step * integral
    return advect_rows(sectioned, sector_depth, cell_offset, fraction)


MESH = pl.DeviceIdType.MESH
ROWS = 8
LAG = 3
FORWARD_AFTER = 24


def sweep_kernel(
    order_hbm,
    reaction_hbm,
    diff_hbm,
    init_hbm,
    states_hbm,
    depth_hbm,
    offset_hbm,
    frac_hbm,
    out_ref,
    order_ref,
    reaction_ref,
    diff_ref,
    quad_ref,
    init_ref,
    states_ref,
    depth_ref,
    offset_ref,
    frac_ref,
    edge,
    part,
    part_in,
    sect,
    near_out,
    far_out,
    near_in,
    far_in,
    ready,
    row_depth,
    row_offset,
    row_frac,
    load_s,
    edge_s,
    edge_r,
    part_s,
    part_r,
    sect_s,
    sect_r,
    near_s,
    near_r,
    far_s,
    far_r,
    ready_s,
    ready_r,
):
    slots, tracers, _, nlat, cells = states_ref.shape
    blocks = nlat // ROWS
    chunks = 2 * blocks
    pieces = chunks * slots
    lev = lax.axis_index("lev")
    node = lax.axis_index("node")
    lon = lax.axis_index("lon")
    half = lon // 2
    par = lon % 2
    mate = half * 2 + (1 - par)
    middle = (lon == 1) | (lon == 2)
    border = (lon == 0) | (lon == 3)

    loads = [
        pltpu.make_async_copy(source, target, load_s.at[i])
        for i, (source, target) in enumerate(
            (
                (states_hbm, states_ref),
                (order_hbm, order_ref),
                (reaction_hbm, reaction_ref),
                (diff_hbm, diff_ref),
                (init_hbm, init_ref),
                (depth_hbm, depth_ref),
                (offset_hbm, offset_ref),
                (frac_hbm, frac_ref),
            )
        )
    ]
    for load in loads:
        load.start()

    barrier = pltpu.get_barrier_semaphore()
    pl.semaphore_signal(barrier, inc=1, device_id={"lev": 1 - lev}, device_id_type=MESH)
    pl.semaphore_signal(barrier, inc=1, device_id={"node": 1 - node}, device_id_type=MESH)
    pl.semaphore_signal(barrier, inc=1, device_id={"lon": mate}, device_id_type=MESH)

    @pl.when(middle)
    def _():
        pl.semaphore_signal(barrier, inc=1, device_id={"lon": 3 - lon}, device_id_type=MESH)

    table = lobatto_table()
    for m in range(NODES):
        for n in range(NODES):
            quad_ref[m, n] = jnp.float32(table[m, n])

    pl.semaphore_wait(barrier, jnp.where(middle, 4, 3))

    def place(c):
        block = c // 2
        level = jnp.where(c % 2 == 0, lev, 1 - lev)
        return block, level, pl.ds(pl.multiple_of(block * ROWS, ROWS), ROWS)

    def edge_copy(block):
        rows = pl.ds(pl.multiple_of(block * ROWS, ROWS), ROWS)
        return pltpu.make_async_remote_copy(
            src_ref=states_ref.at[:, :, 1 - lev, rows, :],
            dst_ref=edge.at[:, :, rows, :],
            send_sem=edge_s.at[block],
            recv_sem=edge_r.at[block],
            device_id={"lev": 1 - lev},
            device_id_type=MESH,
        )

    def part_copy(f):
        return pltpu.make_async_remote_copy(
            src_ref=part.at[f],
            dst_ref=part_in.at[f],
            send_sem=part_s.at[f],
            recv_sem=part_r.at[f],
            device_id={"node": 1 - node},
            device_id_type=MESH,
        )

    def sect_copy(f):
        return pltpu.make_async_remote_copy(
            src_ref=sect.at[par, f],
            dst_ref=sect.at[par, f],
            send_sem=sect_s.at[f],
            recv_sem=sect_r.at[f],
            device_id={"lon": mate},
            device_id_type=MESH,
        )

    def near_copy(f):
        return pltpu.make_async_remote_copy(
            src_ref=near_out.at[f],
            dst_ref=near_in.at[f],
            send_sem=near_s.at[f],
            recv_sem=near_r.at[f],
            device_id={"lon": 3 - lon},
            device_id_type=MESH,
        )

    def far_copy(f):
        return pltpu.make_async_remote_copy(
            src_ref=far_out.at[f],
            dst_ref=far_in.at[f],
            send_sem=far_s.at[f],
            recv_sem=far_r.at[f],
            device_id={"lon": 3 - lon},
            device_id_type=MESH,
        )

    def ready_copy(f):
        _, level, rows = place(f // slots)
        return pltpu.make_async_remote_copy(
            src_ref=ready.at[f],
            dst_ref=out_ref.at[f % slots, :, level, rows, :],
            send_sem=ready_s.at[f],
            recv_sem=ready_r.at[f],
            device_id={"lon": mate},
            device_id_type=MESH,
        )

    loads[0].wait()

    def start_edge(block, carry):
        edge_copy(block).start()
        return carry

    lax.fori_loop(0, blocks, start_edge, 0)
    for load in loads[1:]:
        load.wait()

    def spread_rows():
        diagonal = lax.broadcasted_iota(jnp.int32, (nlat, nlat), 0) == lax.broadcasted_iota(
            jnp.int32, (nlat, nlat), 1
        )
        for a in range(slots):
            for source, target in (
                (depth_ref, row_depth),
                (offset_ref, row_offset),
                (frac_ref, row_frac),
            ):
                line = jnp.broadcast_to(source[a : a + 1, :], (nlat, nlat)).astype(jnp.float32)
                column = jnp.sum(jnp.where(diagonal, line, 0.0), axis=1, keepdims=True)
                target[a] = jnp.broadcast_to(column, (nlat, cells)).astype(target.dtype)

    def tendencies(c):
        block, level, rows = place(c)
        outer = c % 2 == 0

        @pl.when(jnp.logical_not(outer))
        def _():
            edge_copy(block).wait_recv()

        coefficient = diff_ref[level]

        def body(outer):
            tend = []
            for m in range(slots):
                own = [states_ref[m, t, level, rows, :] for t in range(tracers)]
                acts = [jnp.tanh(x) for x in own]
                row = []
                for t in range(tracers):
                    beyond = own[t] if outer else edge[m, t, rows, :]
                    near = states_ref[m, t, 1 - level, rows, :]
                    value = coefficient * (near - 2.0 * own[t] + beyond)
                    for s in range(tracers):
                        value = value + reaction_ref[t, s] * acts[s]
                    row.append(value)
                tend.append(row)
            for target in range(2):
                group = 1 - node if target == 0 else node
                for a in range(slots):
                    f = c * slots + a
                    to = order_ref[group * slots + a]
                    w = [
                        time_step * quad_ref[to, order_ref[node * slots + m]]
                        for m in range(slots)
                    ]
                    for t in range(tracers):
                        value = w[0] * tend[0][t]
                        for m in range(1, slots):
                            value = value + w[m] * tend[m][t]
                        if target == 0:
                            part[f, t] = value
                        else:
                            sect[par, f, t] = init_ref[t, level, rows, :] + value
                    if target == 0:
                        part_copy(f).start()

        pl.when(outer)(lambda: body(True))
        pl.when(jnp.logical_not(outer))(lambda: body(False))

    def section(f):
        part_copy(f).wait_recv()
        sect[par, f] = sect[par, f] + part_in[f]
        pl.when(border)(lambda: sect_copy(f).start())

    def interpolate(f):
        a = f % slots
        block, level, rows = place(f // slots)
        sect_copy(f).wait_recv()
        lanes = lax.broadcasted_iota(jnp.int32, (ROWS, cells), 1)
        depth = row_depth[a, rows, :]
        offset = row_offset[a, rows, :]
        coeffs = cubic_weights(row_frac[a, rows, :])
        picks = [(lanes - offset + k) & (cells - 1) for k in range(-1, 3)]
        reach = [jnp.where(lanes >= offset - k, depth, depth + 1) for k in range(-1, 3)]

        def weights_of(u):
            rel = [(u - e) & 3 for e in reach]
            return [
                [jnp.where(r == source, w, 0.0) for r, w in zip(rel, coeffs)]
                for source in range(2)
            ]

        def total(taps, weights):
            value = None
            for source in range(2):
                for k in range(4):
                    term = weights[source][k] * taps[source][k]
                    value = term if value is None else value + term
            return value

        w_far = weights_of(2 + par)
        w_near = weights_of(3 - par)
        w_mate = weights_of(1 - par)
        w_own = weights_of(par)
        for t in range(tracers):
            taps = [
                [
                    jnp.take_along_axis(
                        sect[source, f, t], p, axis=1, mode="promise_in_bounds"
                    )
                    for p in picks
                ]
                for source in range(2)
            ]
            far_out[f, t] = total(taps, w_far)
            near_out[f, t] = total(taps, w_near)
            ready[f, t] = total(taps, w_mate)
            out_ref[a, t, level, rows, :] = total(taps, w_own)
        far_copy(f).start()
        near_copy(f).start()

    def forward(f):
        far_copy(f).wait_recv()
        ready[f] = ready[f] + far_in[f]
        ready_copy(f).start()

    def finish(f):
        _, level, rows = place(f // slots)
        a = f % slots
        near_copy(f).wait_recv()
        out_ref[a, :, level, rows, :] = out_ref[a, :, level, rows, :] + near_in[f]

    tendencies(0)
    pl.when(middle)(spread_rows)

    def step(i, carry):
        pl.when(i < chunks)(lambda: tendencies(i))

        def fine(a, carry):
            f = (i - 1) * slots + a
            pl.when(f < pieces)(lambda: section(f))

            @pl.when(middle)
            def _():
                g = f - LAG
                pl.when((g >= 0) & (g < pieces))(lambda: interpolate(g))
                late = f - FORWARD_AFTER
                pl.when((late >= 0) & (f % 2 == 0) & (f < pieces))(
                    lambda: forward(late // 2)
                )

            return carry

        lax.fori_loop(0, slots, fine, 0)
        return carry

    lax.fori_loop(1, chunks + 2, step, 0)

    done = (pieces - FORWARD_AFTER + 1) // 2

    @pl.when(middle)
    def _():
        def early(f, carry):
            finish(f)
            return carry

        def rest(f, carry):
            forward(f)
            finish(f)
            return carry

        lax.fori_loop(0, done, early, 0)
        lax.fori_loop(done, pieces, rest, 0)

        def drain(f, carry):
            near_copy(f).wait_send()
            far_copy(f).wait_send()
            ready_copy(f).wait_send()
            return carry

        lax.fori_loop(0, pieces, drain, 0)

    @pl.when(border)
    def _():
        def drain(f, carry):
            sect_copy(f).wait_send()
            ready_copy(f).wait_recv()
            return carry

        lax.fori_loop(0, pieces, drain, 0)

    def drain_part(f, carry):
        part_copy(f).wait_send()
        return carry

    lax.fori_loop(0, pieces, drain_part, 0)

    def drain_edge(block, carry):
        edge_copy(block).wait_send()
        return carry

    lax.fori_loop(0, blocks, drain_edge, 0)


def kernel_shards(
    initial_state,
    node_states,
    node_order,
    sector_depth,
    cell_offset,
    fraction,
    reaction_matrix,
    diffusivity,
):
    slots, tracers, levels, nlat, cells = node_states.shape
    blocks = nlat // ROWS
    pieces = 2 * blocks * slots
    f32 = jnp.float32
    dma = pltpu.SemaphoreType.DMA
    smem_of = lambda x: pltpu.SMEM(x.shape, x.dtype)
    vmem_of = lambda x: pltpu.VMEM(x.shape, x.dtype)
    pieces_of = lambda *lead: pltpu.VMEM((*lead, pieces, tracers, ROWS, cells), f32)
    return pl.pallas_call(
        sweep_kernel,
        out_shape=jax.ShapeDtypeStruct(node_states.shape, f32),
        in_specs=[pl.BlockSpec(memory_space=pl.ANY)] * 8,
        out_specs=pl.BlockSpec(memory_space=pltpu.VMEM),
        scratch_shapes=[
            smem_of(node_order),
            smem_of(reaction_matrix),
            smem_of(diffusivity),
            pltpu.SMEM((NODES, NODES), f32),
            vmem_of(initial_state),
            vmem_of(node_states),
            vmem_of(sector_depth),
            vmem_of(cell_offset),
            vmem_of(fraction),
            pltpu.VMEM((slots, tracers, nlat, cells), f32),
            pieces_of(),
            pieces_of(),
            pieces_of(2),
            pieces_of(),
            pieces_of(),
            pieces_of(),
            pieces_of(),
            pieces_of(),
            pltpu.VMEM((slots, nlat, cells), jnp.int32),
            pltpu.VMEM((slots, nlat, cells), jnp.int32),
            pltpu.VMEM((slots, nlat, cells), f32),
            dma((8,)),
            dma((blocks,)),
            dma((blocks,)),
        ]
        + [dma((pieces,))] * 10,
        compiler_params=pltpu.CompilerParams(
            collective_id=0, has_side_effects=True, vmem_limit_bytes=56 * 1024 * 1024
        ),
    )(
        node_order,
        reaction_matrix,
        diffusivity,
        initial_state,
        node_states,
        sector_depth,
        cell_offset,
        fraction,
    )


def solution(mesh):
    in_specs = (
        P(None, "lev", "run", "lon"),
        P("node", None, "lev", "run", "lon"),
        P(),
        P("node", "run"),
        P("node", "run"),
        P("node", "run"),
        P(),
        P("lev"),
    )
    out_specs = P("node", None, "lev", "run", "lon")
    sizes = dict(mesh.shape)
    small = sizes["lon"] == 4 and sizes["node"] == 2 and sizes["lev"] == 2
    body = kernel_shards if small else shards
    return jax.shard_map(body, mesh=mesh, in_specs=in_specs, out_specs=out_specs, check_vma=False)
```

```python
import jax
import jax.numpy as jnp
import numpy as np
from jax import lax
from jax.experimental import pallas as pl
from jax.experimental.pallas import tpu as pltpu
from jax.sharding import PartitionSpec as P

NODES = 8


time_step = 0.5
lobatto_points = [
    -1.0,
    -0.8717401485096066,
    -0.5917001814331423,
    -0.2092992179024789,
    0.2092992179024789,
    0.5917001814331423,
    0.8717401485096066,
    1.0,
]


def padded_2(array, sides, width):
    for axis, dim in sides:
        size, length = (lax.axis_size(axis), array.shape[dim])
        up = [(i, (i + 1) % size) for i in range(size - 1)]
        down = [(j, i) for i, j in up]
        last = lax.slice_in_dim(array, length - width, length, axis=dim)
        first = lax.slice_in_dim(array, 0, width, axis=dim)
        before = lax.ppermute(last, axis, up)
        after = lax.ppermute(first, axis, down)
        array = jnp.concatenate([before, array, after], axis=dim)
    return array


def passed_along(array, axis, by):
    length = lax.axis_size(axis)
    return lax.ppermute(array, axis, [(i, (i + by) % length) for i in range(length)])


def lobatto_table():
    points = [(value + 1.0) / 2.0 for value in lobatto_points]
    result_rows = [[0.0] * 8 for m in range(8)]
    for j in range(8):
        poly_coeffs = [1.0]
        for k in range(8):
            if k != j:
                factor = 1.0 / (points[j] - points[k])
                grown = [0.0] * (len(poly_coeffs) + 1)
                for i in range(len(poly_coeffs)):
                    grown[i + 1] = grown[i + 1] + poly_coeffs[i] * factor
                    grown[i] = grown[i] - poly_coeffs[i] * points[k] * factor
                poly_coeffs = grown
        for m in range(8):
            total_value = 0.0
            for i in range(len(poly_coeffs)):
                total_value = total_value + poly_coeffs[i] * points[m] ** (i + 1) / (i + 1)
            result_rows[m][j] = total_value
    return np.array(result_rows)


def cubic_weights(fraction):
    return (
        -fraction * (fraction - 1.0) * (fraction - 2.0) / 6.0,
        (fraction + 1.0) * (fraction - 1.0) * (fraction - 2.0) / 2.0,
        -(fraction + 1.0) * fraction * (fraction - 2.0) / 2.0,
        (fraction + 1.0) * fraction * (fraction - 1.0) / 6.0,
    )


def section_matrix(node_order):
    onehot = (node_order[:, None] == jnp.arange(NODES, dtype=jnp.int32)[None, :]).astype(
        jnp.float32
    )
    quad_values = jnp.asarray(lobatto_table(), jnp.float32)
    left = jnp.dot(onehot, quad_values, precision=lax.Precision.HIGHEST)
    return jnp.dot(left, onehot.T, precision=lax.Precision.HIGHEST)


def tendency_of(states, reaction_matrix, diffusivity):
    level_count = states.shape[2]
    padded = padded_2(states, (("lev", 2),), 1)
    level_pos = lax.axis_index("lev")
    level_last = lax.axis_size("lev") - 1
    below = padded[:, :, :level_count]
    above = padded[:, :, 2:]
    bottom_level = jnp.where(level_pos == 0, states[:, :, :1], below[:, :, :1])
    below = jnp.concatenate([bottom_level, below[:, :, 1:]], axis=2)
    top_level = jnp.where(
        level_pos == level_last, states[:, :, level_count - 1 :], above[:, :, level_count - 1 :]
    )
    above = jnp.concatenate([above[:, :, : level_count - 1], top_level], axis=2)
    curvature = above - 2.0 * states + below
    reaction = jnp.einsum(
        "ts,mslyx->mtlyx", reaction_matrix, jnp.tanh(states), precision=lax.Precision.HIGHEST
    )
    return reaction + diffusivity[None, None, :, None, None] * curvature


def shifted_window(window, starts, length):
    starts = starts[:, None, None, :, None]
    bit = 1
    while bit < length:
        window = jnp.where((starts & bit) != 0, jnp.roll(window, -bit, axis=4), window)
        bit *= 2
    return window


def advect_rows(sectioned, sector_depth, cell_offset, fraction):
    sector_cells = sectioned.shape[4]
    reach_max = min(4, lax.axis_size("lon") - 2) + 1
    depth_cells = sector_depth[:, None, None, :, None]
    nearer = jnp.where(depth_cells == 0, sectioned, 0.0)
    farther = jnp.zeros_like(sectioned)
    previous = sectioned
    for distance in range(1, reach_max + 1):
        source = previous
        arrived = passed_along(source, "lon", 1)
        previous = arrived
        nearer = nearer + jnp.where(depth_cells == distance, arrived, 0.0)
        farther = farther + jnp.where(depth_cells + 1 == distance, arrived, 0.0)
    window = jnp.concatenate([farther, nearer], axis=4)
    starts = sector_cells - cell_offset - 1
    pieces = shifted_window(window, starts, sector_cells)
    coeffs = cubic_weights(fraction)
    result = jnp.zeros_like(sectioned)
    for stencil in range(4):
        result = (
            result
            + coeffs[stencil][:, None, None, :, None]
            * pieces[:, :, :, :, stencil : stencil + sector_cells]
        )
    return result


def shards(
    initial_state,
    node_states,
    node_order,
    sector_depth,
    cell_offset,
    fraction,
    reaction_matrix,
    diffusivity,
):
    slots = node_states.shape[0]
    weights = section_matrix(node_order)
    node_pos = lax.axis_index("node")
    tendency = tendency_of(node_states, reaction_matrix, diffusivity)
    own_rows = lax.dynamic_slice_in_dim(weights, node_pos * slots, slots, 0)
    integral = jnp.einsum(
        "mj,jtlyx->mtlyx",
        own_rows,
        lax.all_gather(tendency, "node", axis=0, tiled=True),
        precision=lax.Precision.HIGHEST,
    )
    sectioned = initial_state[None] + time_step * integral
    return advect_rows(sectioned, sector_depth, cell_offset, fraction)


MESH = pl.DeviceIdType.MESH
ROWS = 8
LAG = 3
FORWARD_LAG = 12
NEAR_EVERY = 4


def sweep_kernel(
    order_hbm,
    reaction_hbm,
    diff_hbm,
    init_hbm,
    states_hbm,
    depth_hbm,
    offset_hbm,
    frac_hbm,
    out_ref,
    order_ref,
    reaction_ref,
    diff_ref,
    quad_ref,
    init_ref,
    states_ref,
    depth_ref,
    offset_ref,
    frac_ref,
    edge,
    part,
    part_in,
    sect,
    near_out,
    far_out,
    near_in,
    far_in,
    ready,
    result,
    row_depth,
    row_offset,
    row_frac,
    load_s,
    edge_s,
    edge_r,
    part_s,
    part_r,
    sect_s,
    sect_r,
    near_s,
    near_r,
    far_s,
    far_r,
    ready_s,
    ready_r,
    result_s,
):
    slots, tracers, _, nlat, cells = states_ref.shape
    blocks = nlat // ROWS
    chunks = 2 * blocks
    pieces = chunks * slots
    lev = lax.axis_index("lev")
    node = lax.axis_index("node")
    lon = lax.axis_index("lon")
    half = lon // 2
    par = lon % 2
    mate = half * 2 + (1 - par)
    middle = (lon == 1) | (lon == 2)
    border = (lon == 0) | (lon == 3)

    loads = [
        pltpu.make_async_copy(source, target, load_s.at[i])
        for i, (source, target) in enumerate(
            (
                (states_hbm, states_ref),
                (order_hbm, order_ref),
                (reaction_hbm, reaction_ref),
                (diff_hbm, diff_ref),
                (init_hbm, init_ref),
                (depth_hbm, depth_ref),
                (offset_hbm, offset_ref),
                (frac_hbm, frac_ref),
            )
        )
    ]
    for load in loads:
        load.start()

    barrier = pltpu.get_barrier_semaphore()
    pl.semaphore_signal(barrier, inc=1, device_id={"lev": 1 - lev}, device_id_type=MESH)
    pl.semaphore_signal(barrier, inc=1, device_id={"node": 1 - node}, device_id_type=MESH)
    pl.semaphore_signal(barrier, inc=1, device_id={"lon": mate}, device_id_type=MESH)

    @pl.when(middle)
    def _():
        pl.semaphore_signal(barrier, inc=1, device_id={"lon": 3 - lon}, device_id_type=MESH)

    table = lobatto_table()
    for m in range(NODES):
        for n in range(NODES):
            quad_ref[m, n] = jnp.float32(table[m, n])

    pl.semaphore_wait(barrier, jnp.where(middle, 4, 3))

    def place(c):
        block = c // 2
        level = jnp.where(c % 2 == 0, lev, 1 - lev)
        return block, level, pl.ds(pl.multiple_of(block * ROWS, ROWS), ROWS)

    def edge_copy(block):
        rows = pl.ds(pl.multiple_of(block * ROWS, ROWS), ROWS)
        return pltpu.make_async_remote_copy(
            src_ref=states_ref.at[:, :, 1 - lev, rows, :],
            dst_ref=edge.at[:, :, rows, :],
            send_sem=edge_s.at[block],
            recv_sem=edge_r.at[block],
            device_id={"lev": 1 - lev},
            device_id_type=MESH,
        )

    def part_copy(f):
        return pltpu.make_async_remote_copy(
            src_ref=part.at[f],
            dst_ref=part_in.at[f],
            send_sem=part_s.at[f],
            recv_sem=part_r.at[f],
            device_id={"node": 1 - node},
            device_id_type=MESH,
        )

    def sect_copy(f):
        return pltpu.make_async_remote_copy(
            src_ref=sect.at[par, f],
            dst_ref=sect.at[par, f],
            send_sem=sect_s.at[f],
            recv_sem=sect_r.at[f],
            device_id={"lon": mate},
            device_id_type=MESH,
        )

    def near_copy(f):
        return pltpu.make_async_remote_copy(
            src_ref=near_out.at[f],
            dst_ref=near_in.at[f],
            send_sem=near_s.at[f],
            recv_sem=near_r.at[f],
            device_id={"lon": 3 - lon},
            device_id_type=MESH,
        )

    def far_copy(f):
        return pltpu.make_async_remote_copy(
            src_ref=far_out.at[f],
            dst_ref=far_in.at[f],
            send_sem=far_s.at[f],
            recv_sem=far_r.at[f],
            device_id={"lon": 3 - lon},
            device_id_type=MESH,
        )

    def ready_copy(f):
        _, level, rows = place(f // slots)
        return pltpu.make_async_remote_copy(
            src_ref=ready.at[f],
            dst_ref=out_ref.at[f % slots, :, level, rows, :],
            send_sem=ready_s.at[f],
            recv_sem=ready_r.at[f],
            device_id={"lon": mate},
            device_id_type=MESH,
        )

    loads[0].wait()

    def start_edge(block, carry):
        edge_copy(block).start()
        return carry

    lax.fori_loop(0, blocks, start_edge, 0)
    for load in loads[1:]:
        load.wait()

    def spread_rows():
        diagonal = lax.broadcasted_iota(jnp.int32, (nlat, nlat), 0) == lax.broadcasted_iota(
            jnp.int32, (nlat, nlat), 1
        )
        for a in range(slots):
            for source, target in (
                (depth_ref, row_depth),
                (offset_ref, row_offset),
                (frac_ref, row_frac),
            ):
                line = jnp.broadcast_to(source[a : a + 1, :], (nlat, nlat)).astype(jnp.float32)
                column = jnp.sum(jnp.where(diagonal, line, 0.0), axis=1, keepdims=True)
                target[a] = jnp.broadcast_to(column, (nlat, cells)).astype(target.dtype)

    def tendencies(c):
        block, level, rows = place(c)
        outer = c % 2 == 0

        @pl.when(jnp.logical_not(outer))
        def _():
            edge_copy(block).wait_recv()

        coefficient = diff_ref[level]

        def body(outer):
            tend = []
            for m in range(slots):
                own = [states_ref[m, t, level, rows, :] for t in range(tracers)]
                acts = [jnp.tanh(x) for x in own]
                row = []
                for t in range(tracers):
                    beyond = own[t] if outer else edge[m, t, rows, :]
                    near = states_ref[m, t, 1 - level, rows, :]
                    value = coefficient * (near - 2.0 * own[t] + beyond)
                    for s in range(tracers):
                        value = value + reaction_ref[t, s] * acts[s]
                    row.append(value)
                tend.append(row)
            for target in range(2):
                group = 1 - node if target == 0 else node
                for a in range(slots):
                    f = c * slots + a
                    to = order_ref[group * slots + a]
                    w = [
                        time_step * quad_ref[to, order_ref[node * slots + m]]
                        for m in range(slots)
                    ]
                    for t in range(tracers):
                        value = w[0] * tend[0][t]
                        for m in range(1, slots):
                            value = value + w[m] * tend[m][t]
                        if target == 0:
                            part[f, t] = value
                        else:
                            sect[par, f, t] = init_ref[t, level, rows, :] + value
                    if target == 0:
                        part_copy(f).start()

        pl.when(outer)(lambda: body(True))
        pl.when(jnp.logical_not(outer))(lambda: body(False))

    def section(f):
        part_copy(f).wait_recv()
        sect[par, f] = sect[par, f] + part_in[f]
        pl.when(border)(lambda: sect_copy(f).start())

    def interpolate(f):
        a = f % slots
        _, _, rows = place(f // slots)
        sect_copy(f).wait_recv()
        lanes = lax.broadcasted_iota(jnp.int32, (ROWS, cells), 1)
        depth = row_depth[a, rows, :]
        offset = row_offset[a, rows, :]
        coeffs = cubic_weights(row_frac[a, rows, :])
        picks = [(lanes - offset + k) & (cells - 1) for k in range(-1, 3)]
        reach = [jnp.where(lanes >= offset - k, depth, depth + 1) for k in range(-1, 3)]

        def weights_of(u):
            rel = [(u - e) & 3 for e in reach]
            return [
                [jnp.where(r == source, w, 0.0) for r, w in zip(rel, coeffs)]
                for source in range(2)
            ]

        def total(taps, weights):
            value = None
            for source in range(2):
                for k in range(4):
                    term = weights[source][k] * taps[source][k]
                    value = term if value is None else value + term
            return value

        w_far = weights_of(2 + par)
        w_near = weights_of(3 - par)
        w_mate = weights_of(1 - par)
        w_own = weights_of(par)
        for t in range(tracers):
            taps = [
                [
                    jnp.take_along_axis(
                        sect[source, f, t], p, axis=1, mode="promise_in_bounds"
                    )
                    for p in picks
                ]
                for source in range(2)
            ]
            far_out[f, t] = total(taps, w_far)
            near_out[f, t] = total(taps, w_near)
            ready[f, t] = total(taps, w_mate)
            result[f, t] = total(taps, w_own)
        far_copy(f).start()
        pl.when(f % NEAR_EVERY == 0)(lambda: near_copy(f // NEAR_EVERY).start())

    def forward(f):
        far_copy(f).wait_recv()
        ready[f] = ready[f] + far_in[f]
        ready_copy(f).start()

    def result_copy(f):
        _, level, rows = place(f // slots)
        return pltpu.make_async_copy(
            result.at[f], out_ref.at[f % slots, :, level, rows, :], result_s.at[f]
        )

    def finish(f):
        near_copy(f).wait_recv()
        result[f] = result[f] + near_in[f]
        result_copy(f).start()

    tendencies(0)
    pl.when(middle)(spread_rows)

    def step(i, carry):
        pl.when(i < chunks)(lambda: tendencies(i))

        def fine(a, carry):
            f = (i - 1) * slots + a
            pl.when(f < pieces)(lambda: section(f))

            @pl.when(middle)
            def _():
                g = f - LAG
                pl.when((g >= 0) & (g < pieces))(lambda: interpolate(g))
                late = f - FORWARD_LAG
                pl.when((late >= 0) & (f < pieces))(lambda: forward(late))

            return carry

        lax.fori_loop(0, slots, fine, 0)
        return carry

    lax.fori_loop(1, chunks + 2, step, 0)

    @pl.when(middle)
    def _():
        def start_near(f, carry):
            near_copy(f).start()
            return carry

        def forward_rest(f, carry):
            forward(f)
            return carry

        def finish_all(f, carry):
            finish(f)
            return carry

        lax.fori_loop((pieces + NEAR_EVERY - 1) // NEAR_EVERY, pieces, start_near, 0)
        lax.fori_loop(pieces - FORWARD_LAG, pieces, forward_rest, 0)
        lax.fori_loop(0, pieces, finish_all, 0)

        def drain(f, carry):
            near_copy(f).wait_send()
            far_copy(f).wait_send()
            ready_copy(f).wait_send()
            result_copy(f).wait()
            return carry

        lax.fori_loop(0, pieces, drain, 0)

    @pl.when(border)
    def _():
        def drain(f, carry):
            sect_copy(f).wait_send()
            ready_copy(f).wait_recv()
            return carry

        lax.fori_loop(0, pieces, drain, 0)

    def drain_part(f, carry):
        part_copy(f).wait_send()
        return carry

    lax.fori_loop(0, pieces, drain_part, 0)

    def drain_edge(block, carry):
        edge_copy(block).wait_send()
        return carry

    lax.fori_loop(0, blocks, drain_edge, 0)


def kernel_shards(
    initial_state,
    node_states,
    node_order,
    sector_depth,
    cell_offset,
    fraction,
    reaction_matrix,
    diffusivity,
):
    slots, tracers, levels, nlat, cells = node_states.shape
    blocks = nlat // ROWS
    pieces = 2 * blocks * slots
    f32 = jnp.float32
    dma = pltpu.SemaphoreType.DMA
    smem_of = lambda x: pltpu.SMEM(x.shape, x.dtype)
    vmem_of = lambda x: pltpu.VMEM(x.shape, x.dtype)
    pieces_of = lambda *lead: pltpu.VMEM((*lead, pieces, tracers, ROWS, cells), f32)
    return pl.pallas_call(
        sweep_kernel,
        out_shape=jax.ShapeDtypeStruct(node_states.shape, f32),
        in_specs=[pl.BlockSpec(memory_space=pl.ANY)] * 8,
        out_specs=pl.BlockSpec(memory_space=pl.ANY),
        scratch_shapes=[
            smem_of(node_order),
            smem_of(reaction_matrix),
            smem_of(diffusivity),
            pltpu.SMEM((NODES, NODES), f32),
            vmem_of(initial_state),
            vmem_of(node_states),
            vmem_of(sector_depth),
            vmem_of(cell_offset),
            vmem_of(fraction),
            pltpu.VMEM((slots, tracers, nlat, cells), f32),
            pieces_of(),
            pieces_of(),
            pieces_of(2),
            pieces_of(),
            pieces_of(),
            pieces_of(),
            pieces_of(),
            pieces_of(),
            pieces_of(),
            pltpu.VMEM((slots, nlat, cells), jnp.int32),
            pltpu.VMEM((slots, nlat, cells), jnp.int32),
            pltpu.VMEM((slots, nlat, cells), f32),
            dma((8,)),
            dma((blocks,)),
            dma((blocks,)),
        ]
        + [dma((pieces,))] * 11,
        compiler_params=pltpu.CompilerParams(
            collective_id=0, has_side_effects=True, vmem_limit_bytes=56 * 1024 * 1024
        ),
    )(
        node_order,
        reaction_matrix,
        diffusivity,
        initial_state,
        node_states,
        sector_depth,
        cell_offset,
        fraction,
    )


def solution(mesh):
    in_specs = (
        P(None, "lev", "run", "lon"),
        P("node", None, "lev", "run", "lon"),
        P(),
        P("node", "run"),
        P("node", "run"),
        P("node", "run"),
        P(),
        P("lev"),
    )
    out_specs = P("node", None, "lev", "run", "lon")
    sizes = dict(mesh.shape)
    small = sizes["lon"] == 4 and sizes["node"] == 2 and sizes["lev"] == 2
    body = kernel_shards if small else shards
    return jax.shard_map(body, mesh=mesh, in_specs=in_specs, out_specs=out_specs, check_vma=False)
```
